32 devices in a mesh: band: 4 (over y, x), col: 8 (over z, core).
Axes of the slice: x: 2, y: 2, z: 4, core: 2. Of those that a mesh axis runs over, the one named last changes fastest.
Arguments:
- covariance: float32 [10240, 10240], P('col', 'band'), may hold values from -1 to 10, as said below
- wind_east: float32 [64, 160], replicated, may hold values from -0.25 to 0.25
- wind_north: float32 [64, 160], replicated, may hold values from -0.25 to 0.25
- obs_owner: int32 [3, 128], replicated, may hold values from 0 to 7, as said below
- obs_offset: int32 [3, 128], replicated, may hold values from 0 to 1279
- obs_variance: float32 [3, 128], replicated, may hold values from 0.3 to 3
Outputs:
- analysis: float32 [10240, 10240], P('col', 'band')
The draws below stay inside these ranges and needn't reach their ends.
Inputs may be any that keep to these rules, and one draw needn't show every extreme that they name: `covariance`: symmetric positive definite. `obs_owner`: in every batch each slab index appears exactly 16 times.
All inputs are finite; a program needn't handle non-finite values.
Results may differ from the reference program's by a relative error of at most 0.00012.
Values sent between devices are 32-bit elements; how exact they have to be, the bound alone decides.
A program may use at most 128 MiB of HBM per device.

```python
import math
import jax
import jax.numpy as jnp
from jax import lax

LATITUDE_ROWS = 64
LONGITUDE_COLUMNS = 160
NOBS = 128
NBATCH = 3
GRID_POINTS = 10240
SLAB_PTS = 1280
OBS_SLAB = 16


def draw_covariance(key, part):
    first_key, second_key = jax.random.split(jax.random.fold_in(key, 17))
    entries = jax.random.normal(first_key, (GRID_POINTS, GRID_POINTS), jnp.float32)
    scales = jnp.exp(jax.random.uniform(second_key, (GRID_POINTS,), jnp.float32, jnp.log(0.7), jnp.log(1.4)))
    symmetric = (entries + entries.T) * (0.3 / jnp.sqrt(jnp.float32(GRID_POINTS)))
    diagonal = jnp.arange(GRID_POINTS)
    symmetric = symmetric.at[diagonal, diagonal].add(1.0)
    scaled = scales[:, None] * symmetric * scales[None, :]
    return scaled.astype(jnp.float32)


def draw_obs_owner(key, part):
    subkeys = jax.random.split(jax.random.fold_in(key, 29), NBATCH)
    orders = jnp.stack([jax.random.permutation(subkeys[batch_index], NOBS) for batch_index in range(NBATCH)])
    return (orders // OBS_SLAB).astype(jnp.int32)


def plant(result, stream_key, low, high):
    place = [jax.random.randint(jax.random.fold_in(stream_key, axis), (), 0, length) for axis, length in enumerate(result.shape)]
    longest = result.shape.index(max(result.shape))
    beside = place[:longest] + [(place[longest] + 1) % result.shape[longest]] + place[longest + 1:]
    return result.at[tuple(place)].set(low).at[tuple(beside)].set(high)


def setup_inputs(seed: int = 0) -> dict:
    streams_of = jax.random.split(jax.random.key(seed), 7)
    covariance = draw_covariance(jax.random.fold_in(streams_of[6], 71), 0)
    wind_east = jnp.clip(jax.random.uniform(streams_of[1], (LATITUDE_ROWS, LONGITUDE_COLUMNS), jnp.float32, -0.25, 0.25), -0.25, 0.25)
    wind_north = jnp.clip(jax.random.uniform(streams_of[2], (LATITUDE_ROWS, LONGITUDE_COLUMNS), jnp.float32, -0.25, 0.25), -0.25, 0.25)
    obs_owner = draw_obs_owner(jax.random.fold_in(streams_of[6], 71), 0)
    obs_offset = plant(jax.random.randint(streams_of[4], (NBATCH, NOBS), 0, SLAB_PTS), jax.random.fold_in(streams_of[4], 1), 0, SLAB_PTS - 1).astype(jnp.int32)
    obs_variance = jnp.clip(jnp.exp(jax.random.uniform(streams_of[5], (NBATCH, NOBS), jnp.float32, math.log(0.3), math.log(3.0))), 0.3, 3.0)
    return dict(covariance=covariance, wind_east=wind_east, wind_north=wind_north, obs_owner=obs_owner, obs_offset=obs_offset, obs_variance=obs_variance)


def advect(padded, east_wind, north_wind, lat_axis):
    length = padded.shape[lat_axis] - 2
    interior = lax.slice_in_dim(padded, 1, length + 1, axis=lat_axis)
    neighbour = jnp.roll(interior, -1, axis=lat_axis + 1)
    east_flux = jnp.maximum(east_wind, 0.0) * interior + jnp.minimum(east_wind, 0.0) * neighbour
    west_flux = jnp.roll(east_flux, 1, axis=lat_axis + 1)
    lower_cells = lax.slice_in_dim(padded, 0, length + 1, axis=lat_axis)
    upper_cells = lax.slice_in_dim(padded, 1, length + 2, axis=lat_axis)
    north_flux = jnp.maximum(north_wind, 0.0) * lower_cells + jnp.minimum(north_wind, 0.0) * upper_cells
    upper_flux = lax.slice_in_dim(north_flux, 1, length + 1, axis=lat_axis)
    lower_flux = lax.slice_in_dim(north_flux, 0, length, axis=lat_axis)
    return interior - (east_flux - west_flux) - (upper_flux - lower_flux)

def north_faces(wind_north):
    lat_count = wind_north.shape[0]
    lat_index = jnp.arange(lat_count)[:, None]
    walled = jnp.where(lat_index < lat_count - 1, wind_north, 0.0)
    return jnp.concatenate([jnp.zeros((1, wind_north.shape[1]), wind_north.dtype), walled], axis=0)

def solve_gain(matrix, right_side):
    factor = jnp.linalg.cholesky(matrix)
    middle = lax.linalg.triangular_solve(factor, right_side, left_side=True, lower=True)
    return lax.linalg.triangular_solve(factor, middle, left_side=True, lower=True, transpose_a=True)

def reference(covariance, wind_east, wind_north, obs_owner, obs_offset, obs_variance):
    face_winds = north_faces(wind_north)
    first_major = covariance.T.reshape(LATITUDE_ROWS, LONGITUDE_COLUMNS, GRID_POINTS)
    padded = jnp.pad(first_major, ((1, 1), (0, 0), (0, 0)))
    advected = advect(padded, wind_east[:, :, None], face_winds[:, :, None], 0)
    block_list = advected.reshape(LATITUDE_ROWS, LONGITUDE_COLUMNS, LATITUDE_ROWS, LONGITUDE_COLUMNS)

    def pass_rows(block_rows):
        grid_rim = jnp.pad(block_rows, ((0, 0), (1, 1), (0, 0)))
        return advect(grid_rim, wind_east[None], face_winds[None], 1)
    predicted_state = lax.map(pass_rows, block_list).reshape(GRID_POINTS, GRID_POINTS)
    for batch_index in range(NBATCH):
        point_list = (obs_owner[batch_index] * SLAB_PTS + obs_offset[batch_index]).astype(jnp.int32)
        column_set = jnp.take(predicted_state, point_list, axis=1)
        observation_rows = jnp.take(predicted_state, point_list, axis=0)
        innovation = jnp.take(column_set, point_list, axis=0) + jnp.diag(obs_variance[batch_index])
        weight_matrix = solve_gain(innovation, observation_rows)
        predicted_state = predicted_state - jnp.dot(column_set.astype(jnp.float32), weight_matrix.astype(jnp.float32), precision=lax.Precision.HIGHEST, preferred_element_type=jnp.float32)
    return predicted_state.T
```

```python
import functools

import jax
import jax.numpy as jnp
from jax import lax
from jax.experimental import pallas as pl
from jax.experimental.pallas import tpu as pltpu
from jax.sharding import PartitionSpec as P

LANES = 128
SUBLANES = 8
PIVOT = 128
VMEM_BYTES = 56 * 1024 * 1024
HIGHEST = lax.Precision.HIGHEST


def stencil_weights(wind_east, wind_north):
    walls = jnp.concatenate([jnp.zeros((1, wind_north.shape[1]), wind_north.dtype), wind_north[:-1], jnp.zeros((1, wind_north.shape[1]), wind_north.dtype)], axis=0)
    west_wind = jnp.roll(wind_east, 1, axis=1)
    upper, lower = walls[1:], walls[:-1]
    own = (
        1.0
        - (jnp.maximum(wind_east, 0.0) - jnp.minimum(west_wind, 0.0))
        - (jnp.maximum(upper, 0.0) - jnp.minimum(lower, 0.0))
    )
    return jnp.stack(
        [own, -jnp.minimum(wind_east, 0.0), jnp.maximum(west_wind, 0.0), -jnp.minimum(upper, 0.0), jnp.maximum(lower, 0.0)]
    )


def lane_weights(weights, lon, strip):
    own, east, west, north, south = weights.reshape(5, -1)
    place = jnp.arange(own.shape[0]) % lon
    first, last = place == 0, place == lon - 1
    here = lambda w: jnp.pad(w, (strip, strip))
    above = lambda w: jnp.pad(w, (strip + lon, strip - lon))
    below = lambda w: jnp.pad(w, (strip - lon, strip + lon))
    rows = [
        here(own),
        here(jnp.where(last, 0.0, east)),
        here(jnp.where(first, 0.0, west)),
        above(north),
        above(jnp.where(first, west, 0.0)),
        below(south),
        below(jnp.where(last, east, 0.0)),
    ]
    return jnp.stack(rows + [jnp.zeros_like(rows[0])])


def along_lanes(cells, lane_ref, lon, strip):
    width = cells.shape[1]
    weight = lambda k: lane_ref[k : k + 1, :]
    east = pltpu.roll(cells, width - 1, 1)
    west = pltpu.roll(cells, 1, 1)
    north = weight(3) * cells + weight(4) * west
    south = weight(5) * cells + weight(6) * east
    total = weight(0) * cells + weight(1) * east + weight(2) * west
    total += pltpu.roll(north, width - lon, 1) + pltpu.roll(south, lon, 1)
    return total[:, strip : width - strip]


def rim_copies(refs, ext_ref, sems, lon, strip):
    cov, left, right, top, bottom, top_ends, bottom_ends = refs
    rows, band = cov.shape
    mid, cols = pl.ds(lon, rows), pl.ds(strip, band)
    ends = (pl.ds(0, strip), pl.ds(strip + band, strip))
    high = pl.ds(lon + rows, lon)
    pairs = [
        (left, ext_ref.at[mid, ends[0]]),
        (right, ext_ref.at[mid, ends[1]]),
        (top, ext_ref.at[pl.ds(0, lon), cols]),
        (bottom, ext_ref.at[high, cols]),
    ]
    for side in range(2):
        part = pl.ds(side * strip, strip)
        pairs.append((top_ends.at[:, part], ext_ref.at[pl.ds(0, lon), ends[side]]))
        pairs.append((bottom_ends.at[:, part], ext_ref.at[high, ends[side]]))
    return [pltpu.make_async_copy(src, dst, sems.at[k]) for k, (src, dst) in enumerate(pairs)]


def block_copy(cov, ext_ref, sems, lon, strip, step):
    rows = pl.ds(pl.multiple_of(step * lon, SUBLANES), lon)
    dst = pl.ds(pl.multiple_of((step + 1) * lon, SUBLANES), lon)
    return pltpu.make_async_copy(cov.at[rows, :], ext_ref.at[dst, pl.ds(strip, cov.shape[1])], sems.at[step])


def observed_kernel(lon, strip, count, spots, row_weights, lanes, *rest):
    refs, (out, ext, picked, rim_sems, block_sems) = rest[:7], rest[7:]
    rows = refs[0].shape[0]
    steps = rows // lon
    copies = rim_copies(refs, ext, rim_sems, lon, strip)
    for step in range(steps):
        block_copy(refs[0], ext, block_sems, lon, strip, step).start()
    for copy in copies:
        copy.start()
    picked[...] = jnp.zeros_like(picked)
    for step in range(steps):
        block_copy(refs[0], ext, block_sems, lon, strip, step).wait()
    for copy in copies:
        copy.wait()

    @pl.loop(0, count)
    def _(k):
        spot = spots[k]
        place = lax.rem(spot, lon)
        east = jnp.where(place == lon - 1, spot + 1 - lon, spot + 1)
        west = jnp.where(place == 0, spot + lon - 1, spot - 1)
        total = row_weights[spot] * ext[pl.ds(lon + spot, 1), :]
        for which, row in enumerate((lon + east, lon + west, 2 * lon + spot, spot)):
            total += row_weights[(which + 1) * rows + spot] * ext[pl.ds(row, 1), :]
        picked[pl.ds(k, 1), :] = total

    for group in range(picked.shape[0] // SUBLANES):
        part = pl.ds(group * SUBLANES, SUBLANES)
        out[part, :] = along_lanes(picked[part, :], lanes, lon, strip)


def forecast_kernel(lon, strip, row_weights, lanes, *rest):
    refs, (out, ext, rim_sems, block_sems) = rest[:7], rest[7:]
    steps = refs[0].shape[0] // lon
    step = pl.program_id(0)
    groups = lon // SUBLANES
    copies = rim_copies(refs, ext, rim_sems, lon, strip)
    fetch = functools.partial(block_copy, refs[0], ext, block_sems, lon, strip)

    @pl.when(step == 0)
    def _():
        for copy in copies:
            copy.start()
        for s in range(steps):
            fetch(s).start()
        for copy in copies:
            copy.wait()
        fetch(0).wait()

    @pl.when(step + 1 < steps)
    def _():
        fetch(step + 1).wait()

    base = (step + 1) * lon
    line = lax.broadcasted_iota(jnp.int32, (SUBLANES, ext.shape[1]), 0)
    read = lambda row: ext[pl.ds(pl.multiple_of(row, SUBLANES), SUBLANES), :]

    @pl.loop(0, groups)
    def _(group):
        row = base + group * SUBLANES
        after = base + jnp.where(group == groups - 1, 0, group + 1) * SUBLANES
        before = base + jnp.where(group == 0, groups - 1, group - 1) * SUBLANES
        cells = read(row)
        east = jnp.where(line == SUBLANES - 1, pltpu.roll(read(after), SUBLANES - 1, 0), pltpu.roll(cells, SUBLANES - 1, 0))
        west = jnp.where(line == 0, pltpu.roll(read(before), 1, 0), pltpu.roll(cells, 1, 0))
        part = pl.ds(pl.multiple_of(group * SUBLANES, SUBLANES), SUBLANES)
        factors = row_weights[part, :]
        factor = lambda k: factors[:, k : k + 1]
        total = factor(0) * cells + factor(1) * east + factor(2) * west
        total += factor(3) * read(row + lon) + factor(4) * read(row - lon)
        out[part, :] = along_lanes(total, lanes, lon, strip)


def spread(block, k):
    return jnp.take_along_axis(block, jnp.full(block.shape, k, jnp.int32), axis=1, mode="promise_in_bounds")


def inverse_kernel(source, out, work):
    size = source.shape[0]
    out[...] = source[...]
    sub = lax.broadcasted_iota(jnp.int32, (PIVOT, PIVOT), 0)
    lane = lax.broadcasted_iota(jnp.int32, (PIVOT, PIVOT), 1)
    dot = functools.partial(jnp.dot, precision=HIGHEST, preferred_element_type=jnp.float32)
    for at in range(0, size, PIVOT):
        mine = pl.ds(at, PIVOT)
        work[...] = out[mine, mine]

        def pivot(k, carry):
            block = work[...]
            row = work[pl.ds(k, 1), :]
            column = spread(block, k)
            scale = 1.0 / spread(jnp.broadcast_to(row, (SUBLANES, PIVOT)), k)[:1]
            scaled = row * scale
            on_row, on_lane = sub == k, lane == k
            rest = block - column * scaled
            rest = jnp.where(on_lane, -column * scale, rest)
            work[...] = jnp.where(on_row, jnp.where(on_lane, scale, scaled), rest)
            return carry

        lax.fori_loop(0, PIVOT, pivot, 0)
        inverse = work[...]
        column = out[:, mine]
        row = dot(inverse, out[mine, :])
        out[...] = out[...] - dot(column, row)
        out[:, mine] = -dot(column, inverse)
        out[mine, :] = row
        out[mine, mine] = inverse


def local(covariance, wind_east, wind_north, obs_owner, obs_offset, obs_variance):
    slab, band = covariance.shape
    lat, lon = wind_east.shape
    strip = -(-lon // LANES) * LANES
    strip_rows, slab_rows = band // lon, slab // lon
    col_count, band_count = lax.axis_size("col"), lax.axis_size("band")
    band_id, col_id = lax.axis_index("band"), lax.axis_index("col")

    onward = lambda x, axis, n: lax.ppermute(x, axis, [(i, i + 1) for i in range(n - 1)])
    back = lambda x, axis, n: lax.ppermute(x, axis, [(i + 1, i) for i in range(n - 1)])
    left = onward(covariance[:, band - strip :], "band", band_count)
    right = back(covariance[:, :strip], "band", band_count)
    top = onward(covariance[slab - lon :, :], "col", col_count)
    bottom = back(covariance[:lon, :], "col", col_count)
    ends = lambda rows: jnp.concatenate([left[rows], right[rows]], axis=1)
    top_ends = onward(ends(slice(slab - lon, slab)), "col", col_count)
    bottom_ends = back(ends(slice(0, lon)), "col", col_count)
    rims = (covariance, left, right, top, bottom, top_ends, bottom_ends)

    weights = stencil_weights(wind_east, wind_north)
    lanes = lane_weights(lax.dynamic_slice_in_dim(weights, band_id * strip_rows, strip_rows, 1), lon, strip)
    row_weights = lax.dynamic_slice_in_dim(weights, col_id * slab_rows, slab_rows, 1).reshape(5, slab)

    obs_total = obs_owner.size
    own_count = obs_total // col_count
    owners = obs_owner.reshape(-1)
    order = jnp.arange(obs_total)
    earlier = (owners[:, None] == owners[None, :]) & (order[None, :] < order[:, None])
    places = owners * own_count + jnp.sum(earlier.astype(jnp.int32), axis=1)
    hit = places[None, :] == order[:, None]
    offsets = jnp.sum(jnp.where(hit, obs_offset.reshape(1, -1), 0), axis=1)
    noise = jnp.sum(jnp.where(hit, obs_variance.reshape(1, -1), 0.0), axis=1)
    spots = lax.dynamic_slice_in_dim(offsets, col_id * own_count, own_count, 0)

    ext_shape = pltpu.VMEM((slab + 2 * lon, band + 2 * strip), jnp.float32)
    sems = [pltpu.SemaphoreType.DMA((8,)), pltpu.SemaphoreType.DMA((slab_rows,))]
    anywhere = [pl.BlockSpec(memory_space=pl.ANY)] * 7
    in_smem = pl.BlockSpec(memory_space=pltpu.SMEM)
    in_vmem = pl.BlockSpec(memory_space=pltpu.VMEM)
    params = pltpu.CompilerParams(vmem_limit_bytes=VMEM_BYTES)
    padded = -(-own_count // SUBLANES) * SUBLANES
    observed = pl.pallas_call(
        functools.partial(observed_kernel, lon, strip, own_count),
        out_shape=jax.ShapeDtypeStruct((padded, band), jnp.float32),
        in_specs=[in_smem, in_smem, in_vmem] + anywhere,
        out_specs=in_vmem,
        scratch_shapes=[ext_shape, pltpu.VMEM((padded, band + 2 * strip), jnp.float32)] + sems,
        compiler_params=params,
        cost_estimate=pl.CostEstimate(flops=10**7, bytes_accessed=4 * slab * band, transcendentals=0),
    )(spots, row_weights.reshape(-1), lanes, *rims)[:own_count]

    forecast = pl.pallas_call(
        functools.partial(forecast_kernel, lon, strip),
        grid=(slab_rows,),
        out_shape=jax.ShapeDtypeStruct((slab, band), jnp.float32),
        in_specs=[pl.BlockSpec((lon, 8), lambda s: (s, 0)), pl.BlockSpec((8, band + 2 * strip), lambda s: (0, 0))] + anywhere,
        out_specs=pl.BlockSpec((lon, band), lambda s: (s, 0)),
        scratch_shapes=[ext_shape] + sems,
        compiler_params=params,
        cost_estimate=pl.CostEstimate(flops=30 * slab * band, bytes_accessed=32 * slab * band, transcendentals=0),
    )(jnp.pad(row_weights, ((0, 3), (0, 0))).T, lanes, *rims)

    band_rows = lax.all_gather(observed, "col", axis=0, tiled=True)
    pieces = observed.reshape(own_count, band // slab, slab).transpose(1, 0, 2)
    pieces = lax.all_gather(pieces, "band", axis=0, tiled=True)
    slab_part = lax.all_to_all(pieces, "col", 0, 0, tiled=True).reshape(obs_total, slab)
    chosen = (spots[:, None] == jnp.arange(slab)[None, :]).astype(jnp.float32)
    own_block = lax.dot_general(chosen, slab_part, (((1,), (1,)), ((), ())), precision=HIGHEST, preferred_element_type=jnp.float32)
    innovation = lax.all_gather(own_block, "col", axis=0, tiled=True)
    innovation = jnp.where(order[:, None] == order[None, :], innovation + noise[:, None], innovation)

    inverse = pl.pallas_call(
        inverse_kernel,
        out_shape=jax.ShapeDtypeStruct(innovation.shape, jnp.float32),
        in_specs=[in_vmem],
        out_specs=in_vmem,
        scratch_shapes=[pltpu.VMEM((PIVOT, PIVOT), jnp.float32)],
        compiler_params=params,
    )(innovation)
    gain = jnp.dot(inverse, slab_part, precision=HIGHEST, preferred_element_type=jnp.float32)
    change = lax.dot_general(gain, band_rows, (((0,), (0,)), ((), ())), precision=lax.Precision.HIGH, preferred_element_type=jnp.float32)
    return forecast - change


def solution(mesh):
    return jax.shard_map(
        local,
        mesh=mesh,
        in_specs=(P("col", "band"), P(), P(), P(), P(), P()),
        out_specs=P("col", "band"),
        check_vma=False,
    )
```

```python
import functools

import jax
import jax.numpy as jnp
from jax import lax
from jax.experimental import pallas as pl
from jax.experimental.pallas import tpu as pltpu
from jax.sharding import PartitionSpec as P

LANES = 128
SUBLANES = 8
PIVOT = 128
VMEM_BYTES = 56 * 1024 * 1024
HIGHEST = lax.Precision.HIGHEST


def stencil_weights(wind_east, wind_north):
    walls = jnp.concatenate([jnp.zeros((1, wind_north.shape[1]), wind_north.dtype), wind_north[:-1], jnp.zeros((1, wind_north.shape[1]), wind_north.dtype)], axis=0)
    west_wind = jnp.roll(wind_east, 1, axis=1)
    upper, lower = walls[1:], walls[:-1]
    own = (
        1.0
        - (jnp.maximum(wind_east, 0.0) - jnp.minimum(west_wind, 0.0))
        - (jnp.maximum(upper, 0.0) - jnp.minimum(lower, 0.0))
    )
    return jnp.stack(
        [own, -jnp.minimum(wind_east, 0.0), jnp.maximum(west_wind, 0.0), -jnp.minimum(upper, 0.0), jnp.maximum(lower, 0.0)]
    )


def lane_weights(weights, lon, strip):
    own, east, west, north, south = weights.reshape(5, -1)
    place = jnp.arange(own.shape[0]) % lon
    first, last = place == 0, place == lon - 1
    here = lambda w: jnp.pad(w, (strip, strip))
    above = lambda w: jnp.pad(w, (strip + lon, strip - lon))
    below = lambda w: jnp.pad(w, (strip - lon, strip + lon))
    rows = [
        here(own),
        here(jnp.where(last, 0.0, east)),
        here(jnp.where(first, 0.0, west)),
        above(north),
        above(jnp.where(first, west, 0.0)),
        below(south),
        below(jnp.where(last, east, 0.0)),
    ]
    return jnp.stack(rows + [jnp.zeros_like(rows[0])])


def along_lanes(cells, lane_ref, lon, strip):
    width = cells.shape[1]
    weight = lambda k: lane_ref[k : k + 1, :]
    east = pltpu.roll(cells, width - 1, 1)
    west = pltpu.roll(cells, 1, 1)
    north = weight(3) * cells + weight(4) * west
    south = weight(5) * cells + weight(6) * east
    total = weight(0) * cells + weight(1) * east + weight(2) * west
    total += pltpu.roll(north, width - lon, 1) + pltpu.roll(south, lon, 1)
    return total[:, strip : width - strip]


def rim_copies(refs, ext_ref, sems, lon, strip):
    cov, left, right, top, bottom, top_ends, bottom_ends = refs
    rows, band = cov.shape
    mid, cols = pl.ds(lon, rows), pl.ds(strip, band)
    ends = (pl.ds(0, strip), pl.ds(strip + band, strip))
    high = pl.ds(lon + rows, lon)
    pairs = [
        (left, ext_ref.at[mid, ends[0]]),
        (right, ext_ref.at[mid, ends[1]]),
        (top, ext_ref.at[pl.ds(0, lon), cols]),
        (bottom, ext_ref.at[high, cols]),
    ]
    for side in range(2):
        part = pl.ds(side * strip, strip)
        pairs.append((top_ends.at[:, part], ext_ref.at[pl.ds(0, lon), ends[side]]))
        pairs.append((bottom_ends.at[:, part], ext_ref.at[high, ends[side]]))
    return [pltpu.make_async_copy(src, dst, sems.at[k]) for k, (src, dst) in enumerate(pairs)]


def block_copy(cov, ext_ref, sems, lon, strip, step):
    rows = pl.ds(pl.multiple_of(step * lon, SUBLANES), lon)
    dst = pl.ds(pl.multiple_of((step + 1) * lon, SUBLANES), lon)
    return pltpu.make_async_copy(cov.at[rows, :], ext_ref.at[dst, pl.ds(strip, cov.shape[1])], sems.at[step])


def observed_kernel(lon, strip, count, spots, row_weights, lanes, *rest):
    refs, (out, ext, picked, rim_sems, block_sems) = rest[:7], rest[7:]
    rows = refs[0].shape[0]
    steps = rows // lon
    copies = rim_copies(refs, ext, rim_sems, lon, strip)
    for step in range(steps):
        block_copy(refs[0], ext, block_sems, lon, strip, step).start()
    for copy in copies:
        copy.start()
    picked[...] = jnp.zeros_like(picked)
    for step in range(steps):
        block_copy(refs[0], ext, block_sems, lon, strip, step).wait()
    for copy in copies:
        copy.wait()

    @pl.loop(0, count)
    def _(k):
        spot = spots[k]
        place = lax.rem(spot, lon)
        east = jnp.where(place == lon - 1, spot + 1 - lon, spot + 1)
        west = jnp.where(place == 0, spot + lon - 1, spot - 1)
        total = row_weights[spot] * ext[pl.ds(lon + spot, 1), :]
        for which, row in enumerate((lon + east, lon + west, 2 * lon + spot, spot)):
            total += row_weights[(which + 1) * rows + spot] * ext[pl.ds(row, 1), :]
        picked[pl.ds(k, 1), :] = total

    for group in range(picked.shape[0] // SUBLANES):
        part = pl.ds(group * SUBLANES, SUBLANES)
        out[part, :] = along_lanes(picked[part, :], lanes, lon, strip)


def forecast_kernel(lon, strip, row_weights, lanes, *rest):
    refs, (out, ext, rim_sems, block_sems) = rest[:7], rest[7:]
    steps = refs[0].shape[0] // lon
    step = pl.program_id(0)
    groups = lon // SUBLANES
    copies = rim_copies(refs, ext, rim_sems, lon, strip)
    fetch = functools.partial(block_copy, refs[0], ext, block_sems, lon, strip)

    @pl.when(step == 0)
    def _():
        for copy in copies:
            copy.start()
        for s in range(steps):
            fetch(s).start()
        for copy in copies:
            copy.wait()
        fetch(0).wait()

    @pl.when(step + 1 < steps)
    def _():
        fetch(step + 1).wait()

    base = (step + 1) * lon
    line = lax.broadcasted_iota(jnp.int32, (SUBLANES, ext.shape[1]), 0)
    read = lambda row: ext[pl.ds(pl.multiple_of(row, SUBLANES), SUBLANES), :]

    @pl.loop(0, groups)
    def _(group):
        row = base + group * SUBLANES
        after = base + jnp.where(group == groups - 1, 0, group + 1) * SUBLANES
        before = base + jnp.where(group == 0, groups - 1, group - 1) * SUBLANES
        cells = read(row)
        east = jnp.where(line == SUBLANES - 1, pltpu.roll(read(after), SUBLANES - 1, 0), pltpu.roll(cells, SUBLANES - 1, 0))
        west = jnp.where(line == 0, pltpu.roll(read(before), 1, 0), pltpu.roll(cells, 1, 0))
        part = pl.ds(pl.multiple_of(group * SUBLANES, SUBLANES), SUBLANES)
        factors = row_weights[part, :]
        factor = lambda k: factors[:, k : k + 1]
        total = factor(0) * cells + factor(1) * east + factor(2) * west
        total += factor(3) * read(row + lon) + factor(4) * read(row - lon)
        out[part, :] = along_lanes(total, lanes, lon, strip)


def spread(block, k):
    return jnp.take_along_axis(block, jnp.full(block.shape, k, jnp.int32), axis=1, mode="promise_in_bounds")


def inverse_kernel(source, out, work):
    size = source.shape[0]
    out[...] = source[...]
    sub = lax.broadcasted_iota(jnp.int32, (PIVOT, PIVOT), 0)
    lane = lax.broadcasted_iota(jnp.int32, (PIVOT, PIVOT), 1)
    dot = functools.partial(jnp.dot, precision=HIGHEST, preferred_element_type=jnp.float32)
    for at in range(0, size, PIVOT):
        mine = pl.ds(at, PIVOT)
        work[...] = out[mine, mine]

        def pivot(k, carry):
            block = work[...]
            row = work[pl.ds(k, 1), :]
            column = spread(block, k)
            scale = 1.0 / spread(jnp.broadcast_to(row, (SUBLANES, PIVOT)), k)[:1]
            scaled = row * scale
            on_row, on_lane = sub == k, lane == k
            rest = block - column * scaled
            rest = jnp.where(on_lane, -column * scale, rest)
            work[...] = jnp.where(on_row, jnp.where(on_lane, scale, scaled), rest)
            return carry

        lax.fori_loop(0, PIVOT, pivot, 0)
        inverse = work[...]
        column = out[:, mine]
        row = dot(inverse, out[mine, :])
        out[...] = out[...] - dot(column, row)
        out[:, mine] = -dot(column, inverse)
        out[mine, :] = row
        out[mine, mine] = inverse


def halves(values):
    high = values.astype(jnp.bfloat16)
    return high, (values - high.astype(jnp.float32)).astype(jnp.bfloat16)


def update_kernel(forecast, gain, rows, out, rows_high, rows_low):
    @pl.when(pl.program_id(0) == 0)
    def _():
        rows_high[...], rows_low[...] = halves(rows[...])

    high, low = halves(gain[...])
    dot = functools.partial(jnp.dot, preferred_element_type=jnp.float32)
    change = dot(high, rows_high[...]) + dot(high, rows_low[...]) + dot(low, rows_high[...])
    out[...] = forecast[...] - change


def local(covariance, wind_east, wind_north, obs_owner, obs_offset, obs_variance):
    slab, band = covariance.shape
    lat, lon = wind_east.shape
    strip = -(-lon // LANES) * LANES
    strip_rows, slab_rows = band // lon, slab // lon
    col_count, band_count = lax.axis_size("col"), lax.axis_size("band")
    band_id, col_id = lax.axis_index("band"), lax.axis_index("col")

    onward = lambda x, axis, n: lax.ppermute(x, axis, [(i, i + 1) for i in range(n - 1)])
    back = lambda x, axis, n: lax.ppermute(x, axis, [(i + 1, i) for i in range(n - 1)])
    left = onward(covariance[:, band - lon :].T, "band", band_count).T
    left = jnp.pad(left, ((0, 0), (strip - lon, 0)))
    right = back(covariance[:, :lon].T, "band", band_count).T
    right = jnp.pad(right, ((0, 0), (0, strip - lon)))
    top = onward(covariance[slab - lon :, :], "col", col_count)
    bottom = back(covariance[:lon, :], "col", col_count)
    ends = lambda rows: jnp.concatenate([left[rows], right[rows]], axis=1)
    top_ends = onward(ends(slice(slab - lon, slab)), "col", col_count)
    bottom_ends = back(ends(slice(0, lon)), "col", col_count)
    rims = (covariance, left, right, top, bottom, top_ends, bottom_ends)

    weights = stencil_weights(wind_east, wind_north)
    lanes = lane_weights(lax.dynamic_slice_in_dim(weights, band_id * strip_rows, strip_rows, 1), lon, strip)
    row_weights = lax.dynamic_slice_in_dim(weights, col_id * slab_rows, slab_rows, 1).reshape(5, slab)

    obs_total = obs_owner.size
    own_count = obs_total // col_count
    owners = obs_owner.reshape(-1)
    order = jnp.arange(obs_total)
    earlier = (owners[:, None] == owners[None, :]) & (order[None, :] < order[:, None])
    places = owners * own_count + jnp.sum(earlier.astype(jnp.int32), axis=1)
    hit = places[None, :] == order[:, None]
    offsets = jnp.sum(jnp.where(hit, obs_offset.reshape(1, -1), 0), axis=1)
    noise = jnp.sum(jnp.where(hit, obs_variance.reshape(1, -1), 0.0), axis=1)
    spots = lax.dynamic_slice_in_dim(offsets, col_id * own_count, own_count, 0)

    ext_shape = pltpu.VMEM((slab + 2 * lon, band + 2 * strip), jnp.float32)
    sems = [pltpu.SemaphoreType.DMA((8,)), pltpu.SemaphoreType.DMA((slab_rows,))]
    anywhere = [pl.BlockSpec(memory_space=pl.ANY)] * 7
    in_smem = pl.BlockSpec(memory_space=pltpu.SMEM)
    in_vmem = pl.BlockSpec(memory_space=pltpu.VMEM)
    params = pltpu.CompilerParams(vmem_limit_bytes=VMEM_BYTES)
    padded = -(-own_count // SUBLANES) * SUBLANES
    observed = pl.pallas_call(
        functools.partial(observed_kernel, lon, strip, own_count),
        out_shape=jax.ShapeDtypeStruct((padded, band), jnp.float32),
        in_specs=[in_smem, in_smem, in_vmem] + anywhere,
        out_specs=in_vmem,
        scratch_shapes=[ext_shape, pltpu.VMEM((padded, band + 2 * strip), jnp.float32)] + sems,
        compiler_params=params,
        cost_estimate=pl.CostEstimate(flops=10**7, bytes_accessed=4 * slab * band, transcendentals=0),
    )(spots, row_weights.reshape(-1), lanes, *rims)[:own_count]

    lanes, observed = lax.optimization_barrier((lanes, observed))
    forecast = pl.pallas_call(
        functools.partial(forecast_kernel, lon, strip),
        grid=(slab_rows,),
        out_shape=jax.ShapeDtypeStruct((slab, band), jnp.float32),
        in_specs=[pl.BlockSpec((lon, 8), lambda s: (s, 0)), pl.BlockSpec((8, band + 2 * strip), lambda s: (0, 0))] + anywhere,
        out_specs=pl.BlockSpec((lon, band), lambda s: (s, 0)),
        scratch_shapes=[ext_shape] + sems,
        compiler_params=params,
        cost_estimate=pl.CostEstimate(flops=30 * slab * band, bytes_accessed=60 * slab * band, transcendentals=0),
    )(jnp.pad(row_weights, ((0, 3), (0, 0))).T, lanes, *rims)

    pieces = observed.reshape(own_count, band // slab, slab).transpose(1, 0, 2)
    pieces = lax.all_gather(pieces, "band", axis=0, tiled=True)
    pieces, forecast = lax.optimization_barrier((pieces, forecast))
    slab_part = lax.all_to_all(pieces, "col", 0, 0, tiled=True).reshape(obs_total, slab)
    chosen = (offsets.reshape(col_count, own_count, 1) == jnp.arange(slab)).astype(jnp.float32)
    own_block = lax.dot_general(pieces, chosen, (((2,), (2,)), ((0,), (0,))), precision=HIGHEST, preferred_element_type=jnp.float32)
    own_block = own_block.transpose(1, 0, 2).reshape(own_count, obs_total)
    innovation = lax.all_gather(own_block, "col", axis=0, tiled=True)
    innovation, observed = lax.optimization_barrier((innovation, observed))
    band_rows = lax.all_gather(observed, "col", axis=0, tiled=True)
    innovation = jnp.where(order[:, None] == order[None, :], innovation + noise[:, None], innovation)

    inverse = pl.pallas_call(
        inverse_kernel,
        out_shape=jax.ShapeDtypeStruct(innovation.shape, jnp.float32),
        in_specs=[in_vmem],
        out_specs=in_vmem,
        scratch_shapes=[pltpu.VMEM((PIVOT, PIVOT), jnp.float32)],
        compiler_params=params,
    )(innovation)
    gain = lax.dot_general(slab_part, inverse, (((0,), (0,)), ((), ())), precision=HIGHEST, preferred_element_type=jnp.float32)
    return pl.pallas_call(
        update_kernel,
        grid=(slab_rows,),
        out_shape=jax.ShapeDtypeStruct((slab, band), jnp.float32),
        in_specs=[
            pl.BlockSpec((lon, band), lambda s: (s, 0)),
            pl.BlockSpec((lon, obs_total), lambda s: (s, 0)),
            pl.BlockSpec((obs_total, band), lambda s: (0, 0)),
        ],
        out_specs=pl.BlockSpec((lon, band), lambda s: (s, 0)),
        scratch_shapes=[pltpu.VMEM((obs_total, band), jnp.bfloat16)] * 2,
        compiler_params=params,
    )(forecast, gain, band_rows)


def solution(mesh):
    return jax.shard_map(
        local,
        mesh=mesh,
        in_specs=(P("col", "band"), P(), P(), P(), P(), P()),
        out_specs=P("col", "band"),
        check_vma=False,
    )
```
